256 devices in a mesh: row: 8 (over z), col: 32 (over x, y, core).
Axes of the slice: x: 4, y: 4, z: 8, core: 2. Of those that a mesh axis runs over, the one named last changes fastest.
Arguments:
- kernel: float32 [12, 1024, 3, 4096], P(None, 'row', None, 'col'), may hold values from -0.25 to 3, as said below
Outputs:
- factored: float32 [12, 1024, 3, 4096], P(None, 'row', None, 'col')
The draws below stay inside these ranges and needn't reach their ends.
Inputs may be any that keep to these rules, and one draw needn't show every extreme that they name: kernel is symmetric positive definite; diagonal entries lie in 2 to 3 and off-diagonal entries in -0.25 to 1.25.
All inputs are finite; a program needn't handle non-finite values.
Results may differ from the reference program's by a relative error of at most 0.0003.
Values sent between devices are 32-bit elements; how exact they have to be, the bound alone decides.
No kernel may reach another device: no remote copies, remote signals or barrier semaphores. Data moves between devices by JAX's collectives and lax.ppermute only.
A program may use at most 64 MiB of HBM per device.

```python
import jax
import jax.numpy as jnp
from jax import lax

TB = 128
TR_DEV = 12
TC_DEV = 3
ORDER = 12288
N_ROW = 8
N_COL = 32


def draw_kernel(key, part):
    key = jax.random.fold_in(key, 11)
    point_key = jax.random.fold_in(key, 1)
    noise_key = jax.random.fold_in(key, 2)
    ridge_key = jax.random.fold_in(key, 3)
    sigma = 0.35 / ORDER ** 0.5
    points = jnp.clip(jax.random.normal(point_key, (ORDER, 16), jnp.float32), -4.0, 4.0)
    base = jnp.clip(jax.random.normal(noise_key, (ORDER, ORDER), jnp.float32), -4.0, 4.0)
    distance = jnp.zeros((ORDER, ORDER), jnp.float32)
    for feature in range(16):
        column = points[:, feature]
        spread = column[:, None] - column[None, :]
        distance = distance + spread * spread
    gaussian = jnp.exp(distance * jnp.float32(-1.0 / 32.0))
    noise = (base + base.T) * (0.70710678 * sigma)
    ridge = jax.random.uniform(ridge_key, (ORDER,), jnp.float32, 1.0, 2.0)
    indices = jnp.arange(ORDER, dtype=jnp.int32)
    matrix = jnp.where(indices[:, None] == indices[None, :], 1.0 + ridge[:, None], gaussian + noise)
    return matrix.reshape(TR_DEV, N_ROW * TB, TC_DEV, N_COL * TB).astype(jnp.float32)


def setup_inputs(seed: int = 0) -> dict:
    arg_keys = jax.random.split(jax.random.key(seed), 2)
    return {
        "kernel": draw_kernel(jax.random.fold_in(arg_keys[1], 71), 0),
    }


def reference(kernel):
    shape = kernel.shape
    matrix = kernel.reshape(ORDER, ORDER)
    for k in range(2):
        begin = k * TB
        end = begin + TB
        lower = jnp.linalg.cholesky(matrix[begin:end, begin:end])
        solved = lax.linalg.triangular_solve(lower, matrix[end:, begin:end], left_side=False, lower=True, transpose_a=True)
        product = jnp.dot(solved, solved.T, precision=lax.Precision.HIGHEST)
        matrix = matrix.at[end:, end:].set(matrix[end:, end:] - product)
        matrix = matrix.at[begin:end, begin:end].set(jnp.tril(lower))
        matrix = matrix.at[end:, begin:end].set(solved)
        matrix = matrix.at[:begin, begin:end].set(jnp.float32(0.0))
        matrix = matrix.at[begin:end, end:].set(jnp.float32(0.0))
    return matrix.reshape(shape)
```

```python
import functools

import jax
import jax.numpy as jnp
from jax import lax
from jax.experimental import pallas as pl
from jax.experimental.pallas import tpu as pltpu
from jax.sharding import PartitionSpec as P

TB = 128
ROWS = 8
SIDE = 4
ROW_TILES = 12
COL_TILES = 3
HIGHEST = lax.Precision.HIGHEST


def col_of(x, y, core):
    return (x * SIDE + y) * 2 + core


def device_of(z, col):
    return z * SIDE * SIDE * 2 + col


def send(value, pairs):
    return lax.ppermute(value, ("row", "col"), pairs)


def inverse_factor(tile, beside):
    lane = lax.broadcasted_iota(jnp.int32, (8, TB), 1)
    sub = lax.broadcasted_iota(jnp.int32, (8, TB), 0)
    groups = TB // 8
    rows = [tile[8 * g : 8 * g + 8, :] for g in range(groups)]

    def across(value, k):
        return jnp.broadcast_to(value[:, k : k + 1], (8, TB))

    def down(value, k):
        return jnp.broadcast_to(value[k : k + 1, :], (8, TB))

    for p in range(groups):
        first = 8 * p
        wide = {g: [across(rows[g], first + k) for k in range(8)] for g in range(p, groups)}
        inside = (lane >= first) & (lane < first + 8)
        rows[p] = jnp.where(inside, jnp.where(lane - first == sub, 1.0, 0.0), rows[p])
        for g in range(p + 1, groups):
            rows[g] = jnp.where(inside, 0.0, rows[g])
        mine = wide[p]
        coef = {}
        scale = []
        top = []
        for k in range(8):
            r = lax.rsqrt(down(mine[k], k))
            scale.append(r)
            column = jnp.where(sub > k, mine[k] * r, 0.0)
            for m in range(k + 1, 8):
                coef[k, m] = down(mine[m], k) * r
                mine[m] = mine[m] - column * coef[k, m]
            u = down(rows[p], k) * r
            top.append(u)
            rows[p] = jnp.where(sub == k, u, rows[p] - column * u)
        for g in range(p + 1, groups):
            columns = []
            for k in range(8):
                value = wide[g][k]
                for m in range(k):
                    value = value - columns[m] * coef[m, k]
                columns.append(value * scale[k])
            total = rows[g]
            for k in range(8):
                total = total - columns[k] * top[k]
            rows[g] = total
        beside(p)
    return jnp.concatenate([jnp.where(lane <= sub + 8 * g, rows[g], 0.0) for g in range(groups)], axis=0)


def halves(value):
    high = value.astype(jnp.bfloat16)
    return high, (value - high.astype(jnp.float32)).astype(jnp.bfloat16)


def product(a, b, transposed):
    dims = (((1,), (1 if transposed else 0,)), ((), ()))
    dot = functools.partial(lax.dot_general, dimension_numbers=dims, preferred_element_type=jnp.float32)
    return dot(a[0], b[0]) + (dot(a[0], b[1]) + dot(a[1], b[0]))


def exact(a, b, transposed=False):
    dims = (((1,), (1 if transposed else 0,)), ((), ()))
    return lax.dot_general(a, b, dims, precision=HIGHEST, preferred_element_type=jnp.float32)


def factor_and_update(
    place, d00, d01, d11, even, odd, near, far, kernel, out, r_high, r_low, block, in_sem, out_sem
):
    my_row, my_col = place[0], place[1]
    my_x = my_col // (2 * SIDE)
    swapped = lax.rem(my_col, 2) != lax.rem(my_row, 2)
    load = pltpu.make_async_copy(kernel, block, in_sem)
    load.start()

    def turn(s):
        piece = lax.rem(my_x - s % SIDE + SIDE, SIDE)
        a = near[piece, s // SIDE]
        b = far[piece, s // SIDE]
        first = jnp.where(swapped, b, a).T
        second = jnp.where(swapped, a, b).T
        for k, value in enumerate((first, second)):
            high, low = halves(value)
            r_high[s * TB : (s + 1) * TB, k * TB : (k + 1) * TB] = high
            r_low[s * TB : (s + 1) * TB, k * TB : (k + 1) * TB] = low

    def nothing(p):
        pass

    def beside(p):
        if p < ROW_TILES:
            turn(p)

    is_odd = lax.rem(my_row, 2) == 1
    a01 = d01[...]
    a10 = jnp.where(is_odd, a01, a01.T)
    inv00 = inverse_factor(d00[...], beside)
    l10 = exact(a10, inv00, transposed=True)
    schur = d11[...] - exact(l10, l10, transposed=True)
    mixed = exact(l10, inv00)
    inv11 = inverse_factor(schur, nothing)
    inv10 = -exact(inv11, mixed)
    inverse = jnp.concatenate(
        [
            jnp.concatenate([inv00, jnp.zeros((TB, TB), jnp.float32)], axis=1),
            jnp.concatenate([inv10, inv11], axis=1),
        ],
        axis=0,
    )
    inv = halves(inverse)
    top = jnp.concatenate(
        [
            jnp.concatenate([even[t] for t in range(COL_TILES)], axis=1),
            jnp.concatenate([odd[t] for t in range(COL_TILES)], axis=1),
        ],
        axis=0,
    )
    right = halves(product(inv, halves(top), False))

    lane = lax.broadcasted_iota(jnp.int32, (TB, TB), 1)
    sub = lax.broadcasted_iota(jnp.int32, (TB, TB), 0)
    load.wait()
    for s in range(ROW_TILES):
        rows = slice(s * TB, (s + 1) * TB)
        left = product((r_high[rows, :], r_low[rows, :]), inv, True)
        update = product(halves(left), right, False)
        for t in range(COL_TILES):
            block[s, t] = block[s, t] - update[:, t * TB : (t + 1) * TB]

        @pl.when(my_col == 0)
        def _():
            block[s, 0] = left[:, :TB]

        @pl.when(my_col == 1)
        def _():
            block[s, 0] = left[:, TB:]

        if s == 0:
            keep = lane <= sub

            @pl.when(my_row < 2)
            def _():
                for t in range(1, COL_TILES):
                    block[0, t] = jnp.zeros((TB, TB), jnp.float32)

                @pl.when((my_col > 1) | (my_row < my_col))
                def _():
                    block[0, 0] = jnp.zeros((TB, TB), jnp.float32)

                @pl.when(my_row == my_col)
                def _():
                    block[0, 0] = jnp.where(keep, block[0, 0], 0.0)

        pltpu.make_async_copy(block.at[s], out.at[s], out_sem.at[s]).start()
    for s in range(ROW_TILES):
        pltpu.make_async_copy(block.at[s], out.at[s], out_sem.at[s]).wait()


def shards(kernel):
    my_row = lax.axis_index("row").astype(jnp.int32)
    my_col = lax.axis_index("col").astype(jnp.int32)
    my_x = my_col // (2 * SIDE)
    my_y = (my_col // 2) % SIDE
    my_core = my_col % 2
    odd_row = my_row % 2 == 1
    tiles = kernel.transpose(0, 2, 1, 3)
    head = tiles[0]

    cols = range(2 * SIDE * SIDE)
    zs = range(ROWS)
    sides = range(SIDE)
    cores = range(2)

    diag = head[0]
    with jax.named_scope("diag_z"):
        got = send(diag, [(device_of(z, c), device_of(z + 4, c)) for z in (0, 1) for c in cores])
        diag = jnp.where((my_row == 4) | (my_row == 5), got, diag)
        got = send(diag, [(device_of(z, c), device_of(z + 2, c)) for z in (0, 1, 4, 5) for c in cores])
        diag = jnp.where(my_row % 4 >= 2, got, diag)
    with jax.named_scope("diag_x"):
        got = send(diag, [(device_of(z, col_of(0, 0, c)), device_of(z, col_of(2, 0, c))) for z in zs for c in cores])
        diag = jnp.where(my_x == 2, got, diag)
        got = send(
            diag,
            [(device_of(z, col_of(x, 0, c)), device_of(z, col_of(x + 1, 0, c))) for z in zs for x in (0, 2) for c in cores],
        )
        diag = jnp.where(my_x % 2 == 1, got, diag)
    with jax.named_scope("diag_y"):
        got = send(
            diag,
            [(device_of(z, col_of(x, 0, c)), device_of(z, col_of(x, 2, c))) for z in zs for x in sides for c in cores],
        )
        diag = jnp.where(my_y == 2, got, diag)
        got = send(
            diag,
            [
                (device_of(z, col_of(x, y, c)), device_of(z, col_of(x, y + 1, c)))
                for z in zs
                for x in sides
                for y in (0, 2)
                for c in cores
            ],
        )
        diag = jnp.where(my_y % 2 == 1, got, diag)
    swap_core = [(device_of(z, c), device_of(z, c ^ 1)) for z in zs for c in cols]
    swap_row = [(device_of(z, c), device_of(z ^ 1, c)) for z in zs for c in cols]
    with jax.named_scope("diag_swap"):
        other = send(diag, swap_core)
        left = jnp.where(my_core == 0, diag, other)
        right = jnp.where(my_core == 0, other, diag)
        mine = jnp.where(odd_row, right, left)
        theirs = send(mine, swap_row)
        d00 = jnp.where(odd_row, theirs, mine)
        d11 = jnp.where(odd_row, mine, theirs)
        d01 = jnp.where(odd_row, left, right)

    with jax.named_scope("cols"):
        part = head
        got = send(part, [(device_of(z, c), device_of(z + 4, c)) for z in (0, 1) for c in cols])
        part = jnp.where((my_row == 4) | (my_row == 5), got, part)
        got = send(part, [(device_of(z, c), device_of(z + 2, c)) for z in (0, 1, 4, 5) for c in cols])
        part = jnp.where(my_row % 4 >= 2, got, part)
        other_part = send(part, swap_row)
        even = jnp.where(odd_row, other_part, part)
        odd = jnp.where(odd_row, part, other_part)

    with jax.named_scope("rows"):
        home = my_row // 2
        piece = send(
            head,
            [(device_of(0, c), device_of(c % ROWS, c)) for c in cols]
            + [(device_of(1, c), device_of(c % ROWS, c ^ 1)) for c in cols],
        )

        def along_y(starts, step):
            return [
                (
                    device_of(z, col_of(x, (z // 2 + start) % SIDE, c)),
                    device_of(z, col_of(x, (z // 2 + start + step) % SIDE, c)),
                )
                for z in zs
                for x in sides
                for start in starts
                for c in cores
            ]

        def along_x(step):
            return [
                (device_of(z, col_of(x, y, c)), device_of(z, col_of((x + step) % SIDE, y, c)))
                for z in zs
                for x in sides
                for y in sides
                for c in cores
            ]

        got = send(piece, along_y((0,), 2))
        piece = jnp.where((my_y - home) % SIDE == 2, got, piece)
        got = send(piece, along_y((0, 2), 1))
        piece = jnp.where((my_y - home) % SIDE % 2 == 1, got, piece)
        up = send(piece, along_x(1))
        down = send(piece, along_x(-1))
        up2 = send(up, along_x(1))
        near = jnp.stack([piece, up, up2, down])
        far = send(near, swap_core)

    place = jnp.stack([my_row, my_col])
    vmem = pl.BlockSpec(memory_space=pltpu.VMEM)
    anywhere = pl.BlockSpec(memory_space=pl.ANY)
    result = pl.pallas_call(
        factor_and_update,
        out_shape=jax.ShapeDtypeStruct(tiles.shape, tiles.dtype),
        in_specs=[pl.BlockSpec(memory_space=pltpu.SMEM)] + [vmem] * 7 + [anywhere],
        out_specs=anywhere,
        scratch_shapes=[
            pltpu.VMEM((ROW_TILES * TB, 2 * TB), jnp.bfloat16),
            pltpu.VMEM((ROW_TILES * TB, 2 * TB), jnp.bfloat16),
            pltpu.VMEM((ROW_TILES, COL_TILES, TB, TB), jnp.float32),
            pltpu.SemaphoreType.DMA,
            pltpu.SemaphoreType.DMA((ROW_TILES,)),
        ],
        compiler_params=pltpu.CompilerParams(vmem_limit_bytes=40 * 1024 * 1024),
        name="factor_and_update",
    )(place, d00, d01, d11, even, odd, near, far, tiles)
    return result.transpose(0, 2, 1, 3)


def solution(mesh):
    return jax.shard_map(
        shards,
        mesh=mesh,
        in_specs=(P(None, "row", None, "col"),),
        out_specs=P(None, "row", None, "col"),
        check_vma=False,
    )
```

```python
import functools

import jax
import jax.numpy as jnp
from jax import lax
from jax.experimental import pallas as pl
from jax.experimental.pallas import tpu as pltpu
from jax.sharding import PartitionSpec as P

TB = 128
ROWS = 8
SIDE = 4
ROW_TILES = 12
COL_TILES = 3
QUARTER = 3
HIGHEST = lax.Precision.HIGHEST


def col_of(x, y, core):
    return (x * SIDE + y) * 2 + core


def device_of(z, col):
    return z * SIDE * SIDE * 2 + col


def send(value, pairs):
    return lax.ppermute(value, ("row", "col"), pairs)


def inverse_factor(tile):
    lane = lax.broadcasted_iota(jnp.int32, (8, TB), 1)
    sub = lax.broadcasted_iota(jnp.int32, (8, TB), 0)
    groups = TB // 8
    rows = [tile[8 * g : 8 * g + 8, :] for g in range(groups)]

    def across(value, k):
        return jnp.broadcast_to(value[:, k : k + 1], (8, TB))

    def down(value, k):
        return jnp.broadcast_to(value[k : k + 1, :], (8, TB))

    for p in range(groups):
        first = 8 * p
        wide = {g: [across(rows[g], first + k) for k in range(8)] for g in range(p, groups)}
        inside = (lane >= first) & (lane < first + 8)
        rows[p] = jnp.where(inside, jnp.where(lane - first == sub, 1.0, 0.0), rows[p])
        for g in range(p + 1, groups):
            rows[g] = jnp.where(inside, 0.0, rows[g])
        mine = wide[p]
        coef = {}
        scale = []
        top = []
        for k in range(8):
            r = lax.rsqrt(down(mine[k], k))
            scale.append(r)
            column = jnp.where(sub > k, mine[k] * r, 0.0)
            for m in range(k + 1, 8):
                coef[k, m] = down(mine[m], k) * r
                mine[m] = mine[m] - column * coef[k, m]
            u = down(rows[p], k) * r
            top.append(u)
            rows[p] = jnp.where(sub == k, u, rows[p] - column * u)
        for g in range(p + 1, groups):
            columns = []
            for k in range(8):
                value = wide[g][k]
                for m in range(k):
                    value = value - columns[m] * coef[m, k]
                columns.append(value * scale[k])
            total = rows[g]
            for k in range(8):
                total = total - columns[k] * top[k]
            rows[g] = total
    return jnp.concatenate([jnp.where(lane <= sub + 8 * g, rows[g], 0.0) for g in range(groups)], axis=0)


def halves(value):
    high = value.astype(jnp.bfloat16)
    return high, (value - high.astype(jnp.float32)).astype(jnp.bfloat16)


def product(a, b, transposed):
    dims = (((1,), (1 if transposed else 0,)), ((), ()))
    dot = functools.partial(lax.dot_general, dimension_numbers=dims, preferred_element_type=jnp.float32)
    return dot(a[0], b[0]) + (dot(a[0], b[1]) + dot(a[1], b[0]))


def exact(a, b, transposed=False):
    dims = (((1,), (1 if transposed else 0,)), ((), ()))
    return lax.dot_general(a, b, dims, precision=HIGHEST, preferred_element_type=jnp.float32)


def first_block(place, own, by_core, by_row, by_both, inv00, mixed, schur):
    odd_row = lax.rem(place[0], 2) == 1
    odd_col = lax.rem(place[1], 2) == 1
    near_row = jnp.where(odd_col, by_core[...], own[...])
    far_row = jnp.where(odd_col, by_both[...], by_row[...])
    near_row_other = jnp.where(odd_col, own[...], by_core[...])
    far_row_other = jnp.where(odd_col, by_row[...], by_both[...])
    a00 = jnp.where(odd_row, far_row, near_row)
    a10 = jnp.where(odd_row, near_row, far_row)
    a11 = jnp.where(odd_row, near_row_other, far_row_other)
    inv = inverse_factor(a00)
    l10 = exact(a10, inv, transposed=True)
    schur[...] = a11 - exact(l10, l10, transposed=True)
    mixed[...] = exact(l10, inv)
    inv00[...] = inv


def second_block(inv00, mixed, schur, high, low):
    inv11 = inverse_factor(schur[...])
    inv10 = -exact(inv11, mixed[...])
    zero = jnp.zeros((TB, TB), jnp.float32)
    for i, line in enumerate(((inv00[...], zero), (inv10, inv11))):
        for j, value in enumerate(line):
            part = slice(i * TB, (i + 1) * TB), slice(j * TB, (j + 1) * TB)
            high[part], low[part] = halves(value)


def update(place, high, low, part, other_part, near, far, kernel, out, block, sem, sems):
    my_row, my_col = place[0], place[1]
    load = pltpu.make_async_copy(kernel, block, sem)
    load.start()
    odd_row = lax.rem(my_row, 2) == 1
    my_x = my_col // (2 * SIDE)
    my_y = lax.rem(my_col // 2, SIDE)
    swapped = lax.rem(my_col, 2) == 1
    inv = high[...], low[...]
    top = jnp.concatenate(
        [
            jnp.concatenate([jnp.where(odd_row, other_part[t], part[t]) for t in range(COL_TILES)], axis=1),
            jnp.concatenate([jnp.where(odd_row, part[t], other_part[t]) for t in range(COL_TILES)], axis=1),
        ],
        axis=0,
    )
    right = halves(product(inv, halves(top), False))
    lane = lax.broadcasted_iota(jnp.int32, (TB, TB), 1)
    sub = lax.broadcasted_iota(jnp.int32, (TB, TB), 0)

    load.wait()
    for quarter in range(SIDE):
        from_x = lax.rem(my_x - quarter + SIDE, SIDE)
        from_y = lax.rem(my_y - quarter + SIDE, SIDE)
        zero = jnp.where(swapped, far[from_x], near[from_x]).reshape(QUARTER * TB, TB)
        one = jnp.where(swapped, near[from_y], far[from_y]).reshape(QUARTER * TB, TB)
        left = product(halves(jnp.concatenate([zero, one], axis=1)), inv, True)
        change = product(halves(left), right, False)
        for i in range(QUARTER):
            s = quarter * QUARTER + i
            rows = slice(i * TB, (i + 1) * TB)
            for t in range(COL_TILES):
                block[s, t] = block[s, t] - change[rows, t * TB : (t + 1) * TB]

            @pl.when(my_col == 0)
            def _():
                block[s, 0] = left[rows, :TB]

            @pl.when(my_col == 1)
            def _():
                block[s, 0] = left[rows, TB:]

            if s == 0:

                @pl.when(my_row < 2)
                def _():
                    for t in range(1, COL_TILES):
                        block[0, t] = jnp.zeros((TB, TB), jnp.float32)

                    @pl.when((my_col > 1) | (my_row < my_col))
                    def _():
                        block[0, 0] = jnp.zeros((TB, TB), jnp.float32)

                    @pl.when(my_row == my_col)
                    def _():
                        block[0, 0] = jnp.where(lane <= sub, block[0, 0], 0.0)

            pltpu.make_async_copy(block.at[s], out.at[s], sems.at[s]).start()
    for s in range(ROW_TILES):
        pltpu.make_async_copy(block.at[s], out.at[s], sems.at[s]).wait()


def after(value, *others):
    return lax.optimization_barrier((value, *others))[0]


def shards(kernel):
    my_row = lax.axis_index("row").astype(jnp.int32)
    my_col = lax.axis_index("col").astype(jnp.int32)
    my_x = my_col // (2 * SIDE)
    my_y = (my_col // 2) % SIDE
    my_core = my_col % 2
    tiles = kernel.transpose(0, 2, 1, 3)
    place = jnp.stack([my_row, my_col])

    zs = range(ROWS)
    sides = range(SIDE)
    cores = range(2)
    cols = range(2 * SIDE * SIDE)

    def at(z, u, v, core):
        return device_of(z, col_of(u, v, core) if core == 0 else col_of(v, u, core))

    def plane_pairs(planes, us, vs, du, dv):
        return [
            (at(z, u, v, c), at(z, (u + du) % SIDE, (v + dv) % SIDE, c)) for z in planes for u in us for v in vs for c in cores
        ]

    def z_pairs(planes, step, columns):
        return [(device_of(z, c), device_of(z + step, c)) for z in planes for c in columns]

    my_u = jnp.where(my_core == 0, my_x, my_y)
    my_v = jnp.where(my_core == 0, my_y, my_x)
    swap_core = [(device_of(z, c), device_of(z, c ^ 1)) for z in zs for c in cols]
    swap_row = [(device_of(z, c), device_of(z ^ 1, c)) for z in zs for c in cols]
    swap_both = [(device_of(z, c), device_of(z ^ 1, c ^ 1)) for z in zs for c in cols]
    low_planes = (0, 1)

    column = tiles[:, 0].reshape(SIDE, QUARTER, TB, TB)
    head = tiles[0]
    diag = lax.optimization_barrier((head[0], column))[0]
    got = send(diag, plane_pairs(low_planes, (0,), (0,), 2, 0))
    quarter1 = send(column[1], plane_pairs(zs, (0,), (0,), 1, 0))
    quarter3 = send(column[3], plane_pairs(zs, (0,), (0,), 3, 0))
    diag1 = jnp.where(my_u == 2, got, diag)

    got = send(diag1, plane_pairs(low_planes, (0, 2), (0,), 1, 0))
    quarter2 = send(after(column[2], diag1), plane_pairs(zs, (0,), (0,), 2, 0))
    part = after(head, diag1)
    part_got = send(part, z_pairs(low_planes, 4, cols))
    diag2 = jnp.where(my_u % 2 == 1, got, diag1)

    got = send(diag2, plane_pairs(low_planes, sides, (0,), 0, 2))
    diag3 = jnp.where(my_v == 2, got, diag2)

    got = send(diag3, plane_pairs(low_planes, sides, (0, 2), 0, 1))
    quarter1, quarter2, quarter3 = (after(q, diag3) for q in (quarter1, quarter2, quarter3))
    piece = jnp.where(my_u == 0, column[0], jnp.where(my_u == 1, quarter1, jnp.where(my_u == 2, quarter2, quarter3)))
    piece1 = send(piece, plane_pairs(zs, sides, (0,), 0, 1))
    diag4 = jnp.where(my_v % 2 == 1, got, diag3)

    got = send(diag4, z_pairs(low_planes, 4, cols))
    piece3 = send(after(piece, diag4), plane_pairs(zs, sides, (0,), 0, 3))
    piece2 = send(after(piece, diag4), plane_pairs(zs, sides, (0,), 0, 2))
    diag5 = jnp.where((my_row == 4) | (my_row == 5), got, diag4)

    got = send(diag5, z_pairs((0, 1, 4, 5), 2, cols))
    part = jnp.where((my_row == 4) | (my_row == 5), after(part_got, diag5), part)
    part_got = send(part, z_pairs((0, 1, 4, 5), 2, cols))
    diag6 = jnp.where(my_row % 4 >= 2, got, diag5)

    by_core, by_row, by_both = send(diag6, swap_core), send(diag6, swap_row), send(diag6, swap_both)
    piece1, piece2, piece3 = (after(q, by_row) for q in (piece1, piece2, piece3))
    piece = jnp.where(my_v == 0, piece, jnp.where(my_v == 1, piece1, jnp.where(my_v == 2, piece2, piece3)))
    across = send(piece, plane_pairs(zs, sides, sides, 2, 0))
    up = send(piece, plane_pairs(zs, sides, sides, 1, 0))
    down = send(piece, plane_pairs(zs, sides, sides, 3, 0))

    part = jnp.where(my_row % 4 >= 2, part_got, part)
    other_part = send(part, swap_row)
    diag6 = after(diag6, part)

    vmem = pl.BlockSpec(memory_space=pltpu.VMEM)
    smem = pl.BlockSpec(memory_space=pltpu.SMEM)
    anywhere = pl.BlockSpec(memory_space=pl.ANY)
    tile = jax.ShapeDtypeStruct((TB, TB), jnp.float32)
    inverse = jax.ShapeDtypeStruct((2 * TB, 2 * TB), jnp.bfloat16)
    inv00, mixed, schur = pl.pallas_call(
        first_block,
        out_shape=[tile] * 3,
        in_specs=[smem] + [vmem] * 4,
        out_specs=[vmem] * 3,
        compiler_params=pltpu.CompilerParams(vmem_limit_bytes=8 * 1024 * 1024),
        name="first_block",
    )(place, diag6, by_core, by_row, by_both)

    up, down, across = (after(q, schur) for q in (up, down, across))
    near = jnp.stack([piece, up, across, down])
    far = send(near, swap_core)
    high, low = pl.pallas_call(
        second_block,
        out_shape=[inverse] * 2,
        in_specs=[vmem] * 3,
        out_specs=[vmem] * 2,
        compiler_params=pltpu.CompilerParams(vmem_limit_bytes=8 * 1024 * 1024),
        name="second_block",
    )(inv00, mixed, schur)

    far, other_part = (after(q, high) for q in (far, other_part))
    result = pl.pallas_call(
        update,
        out_shape=jax.ShapeDtypeStruct(tiles.shape, tiles.dtype),
        in_specs=[smem] + [vmem] * 6 + [anywhere],
        out_specs=anywhere,
        scratch_shapes=[
            pltpu.VMEM((ROW_TILES, COL_TILES, TB, TB), jnp.float32),
            pltpu.SemaphoreType.DMA,
            pltpu.SemaphoreType.DMA((ROW_TILES,)),
        ],
        compiler_params=pltpu.CompilerParams(vmem_limit_bytes=24 * 1024 * 1024),
        name="update",
    )(place, high, low, part, other_part, near, far, tiles)
    return result.transpose(0, 2, 1, 3)


def solution(mesh):
    return jax.shard_map(
        shards,
        mesh=mesh,
        in_specs=(P(None, "row", None, "col"),),
        out_specs=P(None, "row", None, "col"),
        check_vma=False,
    )
```

```python
import functools

import jax
import jax.numpy as jnp
from jax import lax
from jax.experimental import pallas as pl
from jax.experimental.pallas import tpu as pltpu
from jax.sharding import PartitionSpec as P

TB = 128
ROWS = 8
SIDE = 4
ROW_TILES = 12
COL_TILES = 3
QUARTER = 3
COLS = 32
HIGHEST = lax.Precision.HIGHEST


def col_of(x, y, core):
    return (x * SIDE + y) * 2 + core


def device_of(z, col):
    return z * SIDE * SIDE * 2 + col


def send(value, pairs):
    return lax.ppermute(value, ("row", "col"), pairs)


def inverse_factor(tile):
    lane = lax.broadcasted_iota(jnp.int32, (8, TB), 1)
    sub = lax.broadcasted_iota(jnp.int32, (8, TB), 0)
    groups = TB // 8
    rows = [tile[8 * g : 8 * g + 8, :] for g in range(groups)]

    def across(value, k):
        return jnp.broadcast_to(value[:, k : k + 1], (8, TB))

    def down(value, k):
        return jnp.broadcast_to(value[k : k + 1, :], (8, TB))

    for p in range(groups):
        first = 8 * p
        wide = {g: [across(rows[g], first + k) for k in range(8)] for g in range(p, groups)}
        inside = (lane >= first) & (lane < first + 8)
        rows[p] = jnp.where(inside, jnp.where(lane - first == sub, 1.0, 0.0), rows[p])
        for g in range(p + 1, groups):
            rows[g] = jnp.where(inside, 0.0, rows[g])
        mine = wide[p]
        coef = {}
        scale = []
        top = []
        for k in range(8):
            r = lax.rsqrt(down(mine[k], k))
            scale.append(r)
            column = jnp.where(sub > k, mine[k] * r, 0.0)
            for m in range(k + 1, 8):
                coef[k, m] = down(mine[m], k) * r
                mine[m] = mine[m] - column * coef[k, m]
            u = down(rows[p], k) * r
            top.append(u)
            rows[p] = jnp.where(sub == k, u, rows[p] - column * u)
        for g in range(p + 1, groups):
            columns = []
            for k in range(8):
                value = wide[g][k]
                for m in range(k):
                    value = value - columns[m] * coef[m, k]
                columns.append(value * scale[k])
            total = rows[g]
            for k in range(8):
                total = total - columns[k] * top[k]
            rows[g] = total
    return jnp.concatenate([jnp.where(lane <= sub + 8 * g, rows[g], 0.0) for g in range(groups)], axis=0)


def halves(value):
    high = value.astype(jnp.bfloat16)
    return high, (value - high.astype(jnp.float32)).astype(jnp.bfloat16)


def product(a, b, transposed):
    dims = (((1,), (1 if transposed else 0,)), ((), ()))
    dot = functools.partial(lax.dot_general, dimension_numbers=dims, preferred_element_type=jnp.float32)
    return dot(a[0], b[0]) + (dot(a[0], b[1]) + dot(a[1], b[0]))


def exact(a, b, transposed=False):
    dims = (((1,), (1 if transposed else 0,)), ((), ()))
    return lax.dot_general(a, b, dims, precision=HIGHEST, preferred_element_type=jnp.float32)


def first_block(place, own, by_row, by_core, inv00, below, schur):
    odd_row = lax.rem(place[0], 2) == 1
    odd_col = lax.rem(place[1], 2) == 1
    upper = jnp.where(odd_row, by_row[...], own[...])
    lower = jnp.where(odd_row, own[...], by_row[...])
    inv = inverse_factor(jnp.where(odd_col, by_core[...], upper))
    l10 = exact(jnp.where(odd_col, upper.T, lower), inv, transposed=True)
    schur[...] = jnp.where(odd_col, lower, by_core[...]) - exact(l10, l10, transposed=True)
    below[...] = l10
    inv00[...] = inv


def second_block(inv00, below, schur, high, low):
    mixed = exact(below[...], inv00[...])
    inv11 = inverse_factor(schur[...])
    inv10 = -exact(inv11, mixed)
    zero = jnp.zeros((TB, TB), jnp.float32)
    for i, line in enumerate(((inv00[...], zero), (inv10, inv11))):
        for j, value in enumerate(line):
            part = slice(i * TB, (i + 1) * TB), slice(j * TB, (j + 1) * TB)
            high[part], low[part] = halves(value)


def update(place, high, low, part, other_part, near, far, kernel, out, block, sem, sems):
    my_row, my_col = place[0], place[1]
    load = pltpu.make_async_copy(kernel, block, sem)
    load.start()
    odd_row = lax.rem(my_row, 2) == 1
    my_x = my_col // (2 * SIDE)
    my_y = lax.rem(my_col // 2, SIDE)
    swapped = lax.rem(my_col, 2) == 1
    inv = high[...], low[...]
    top = jnp.concatenate(
        [
            jnp.concatenate([jnp.where(odd_row, other_part[t], part[t]) for t in range(COL_TILES)], axis=1),
            jnp.concatenate([jnp.where(odd_row, part[t], other_part[t]) for t in range(COL_TILES)], axis=1),
        ],
        axis=0,
    )
    right = halves(product(inv, halves(top), False))
    lane = lax.broadcasted_iota(jnp.int32, (TB, TB), 1)
    sub = lax.broadcasted_iota(jnp.int32, (TB, TB), 0)

    load.wait()
    for quarter in range(SIDE):
        from_x = lax.rem(my_x - quarter + SIDE, SIDE)
        from_y = lax.rem(my_y - quarter + SIDE, SIDE)
        zero = jnp.where(swapped, far[from_x], near[from_x]).reshape(QUARTER * TB, TB)
        one = jnp.where(swapped, near[from_y], far[from_y]).reshape(QUARTER * TB, TB)
        left = product(halves(jnp.concatenate([zero, one], axis=1)), inv, True)
        change = product(halves(left), right, False)
        for i in range(QUARTER):
            s = quarter * QUARTER + i
            rows = slice(i * TB, (i + 1) * TB)
            for t in range(COL_TILES):
                value = block[s, t] - change[rows, t * TB : (t + 1) * TB]
                if t == 0:
                    panel = jnp.where(my_col == 0, left[rows, :TB], left[rows, TB:])
                    value = jnp.where(my_col < 2, panel, value)
                if s == 0:
                    tile_col = t * COLS + my_col
                    value = jnp.where((my_row < 2) & (tile_col > my_row), 0.0, value)
                    value = jnp.where((my_row < 2) & (tile_col == my_row) & (lane > sub), 0.0, value)
                block[s, t] = value
            pltpu.make_async_copy(block.at[s], out.at[s], sems.at[s]).start()
    for s in range(ROW_TILES):
        pltpu.make_async_copy(block.at[s], out.at[s], sems.at[s]).wait()


def after(value, *others):
    return lax.optimization_barrier((value, *others))[0]


def shards(kernel):
    my_row = lax.axis_index("row").astype(jnp.int32)
    my_col = lax.axis_index("col").astype(jnp.int32)
    my_x = my_col // (2 * SIDE)
    my_y = (my_col // 2) % SIDE
    my_core = my_col % 2
    tiles = kernel.transpose(0, 2, 1, 3)
    place = jnp.stack([my_row, my_col])

    zs = range(ROWS)
    sides = range(SIDE)
    cores = range(2)
    cols = range(2 * SIDE * SIDE)

    def at(z, u, v, core):
        return device_of(z, col_of(u, v, core) if core == 0 else col_of(v, u, core))

    def plane_pairs(planes, us, vs, du, dv):
        return [
            (at(z, u, v, c), at(z, (u + du) % SIDE, (v + dv) % SIDE, c)) for z in planes for u in us for v in vs for c in cores
        ]

    def z_pairs(planes, step, columns):
        return [(device_of(z, c), device_of(z + step, c)) for z in planes for c in columns]

    my_u = jnp.where(my_core == 0, my_x, my_y)
    my_v = jnp.where(my_core == 0, my_y, my_x)
    swap_core = [(device_of(z, c), device_of(z, c ^ 1)) for z in zs for c in cols]
    swap_row = [(device_of(z, c), device_of(z ^ 1, c)) for z in zs for c in cols]
    low_planes = (0, 1)

    column = tiles[:, 0].reshape(SIDE, QUARTER, TB, TB)
    head = tiles[0]
    diag = lax.optimization_barrier((head[0], column))[0]
    got = send(diag, plane_pairs(low_planes, (0,), (0,), 2, 0))
    quarter1 = send(column[1], plane_pairs(zs, (0,), (0,), 1, 0))
    quarter3 = send(column[3], plane_pairs(zs, (0,), (0,), 3, 0))
    diag1 = jnp.where(my_u == 2, got, diag)

    got = send(diag1, plane_pairs(low_planes, (0, 2), (0,), 1, 0))
    quarter2 = send(after(column[2], diag1), plane_pairs(zs, (0,), (0,), 2, 0))
    part = after(head, diag1)
    part_got = send(part, z_pairs(low_planes, 4, cols))
    diag2 = jnp.where(my_u % 2 == 1, got, diag1)

    got = send(diag2, plane_pairs(low_planes, sides, (0,), 0, 2))
    diag3 = jnp.where(my_v == 2, got, diag2)

    got = send(diag3, plane_pairs(low_planes, sides, (0, 2), 0, 1))
    quarter1, quarter2, quarter3 = (after(q, diag3) for q in (quarter1, quarter2, quarter3))
    piece = jnp.where(my_u == 0, column[0], jnp.where(my_u == 1, quarter1, jnp.where(my_u == 2, quarter2, quarter3)))
    far_piece = send(piece, plane_pairs(zs, sides, (0,), 0, 2))
    diag4 = jnp.where(my_v % 2 == 1, got, diag3)

    got = send(diag4, z_pairs(low_planes, 4, cols))
    diag5 = jnp.where((my_row == 4) | (my_row == 5), got, diag4)

    got = send(diag5, z_pairs((0, 1, 4, 5), 2, cols))
    part = jnp.where((my_row == 4) | (my_row == 5), after(part_got, diag5), part)
    part_got = send(part, z_pairs((0, 1, 4, 5), 2, cols))
    diag6 = jnp.where(my_row % 4 >= 2, got, diag5)

    by_row = send(diag6, swap_row)
    by_core = send(jnp.where(my_row % 2 == my_core, diag6, by_row), swap_core)
    piece = jnp.where(my_v == 2, after(far_piece, diag5), piece)
    piece1 = send(piece, plane_pairs(zs, sides, (0, 2), 0, 1))
    piece = jnp.where(my_v % 2 == 1, after(piece1, by_row), piece)
    across = send(piece, plane_pairs(zs, sides, sides, 2, 0))
    up = send(piece, plane_pairs(zs, sides, sides, 1, 0))
    down = send(piece, plane_pairs(zs, sides, sides, 3, 0))

    part = jnp.where(my_row % 4 >= 2, part_got, part)
    other_part = send(part, swap_row)
    diag6 = after(diag6, part)

    vmem = pl.BlockSpec(memory_space=pltpu.VMEM)
    smem = pl.BlockSpec(memory_space=pltpu.SMEM)
    anywhere = pl.BlockSpec(memory_space=pl.ANY)
    tile = jax.ShapeDtypeStruct((TB, TB), jnp.float32)
    inverse = jax.ShapeDtypeStruct((2 * TB, 2 * TB), jnp.bfloat16)
    inv00, below, schur = pl.pallas_call(
        first_block,
        out_shape=[tile] * 3,
        in_specs=[smem] + [vmem] * 3,
        out_specs=[vmem] * 3,
        compiler_params=pltpu.CompilerParams(vmem_limit_bytes=8 * 1024 * 1024),
        name="first_block",
    )(place, diag6, by_row, by_core)

    up, down, across = (after(q, schur) for q in (up, down, across))
    near = jnp.stack([piece, up, across, down])
    far = send(near, swap_core)
    high, low = pl.pallas_call(
        second_block,
        out_shape=[inverse] * 2,
        in_specs=[vmem] * 3,
        out_specs=[vmem] * 2,
        compiler_params=pltpu.CompilerParams(vmem_limit_bytes=8 * 1024 * 1024),
        name="second_block",
    )(inv00, below, schur)

    far, other_part = (after(q, high) for q in (far, other_part))
    result = pl.pallas_call(
        update,
        out_shape=jax.ShapeDtypeStruct(tiles.shape, tiles.dtype),
        in_specs=[smem] + [vmem] * 6 + [anywhere],
        out_specs=anywhere,
        scratch_shapes=[
            pltpu.VMEM((ROW_TILES, COL_TILES, TB, TB), jnp.float32),
            pltpu.SemaphoreType.DMA,
            pltpu.SemaphoreType.DMA((ROW_TILES,)),
        ],
        compiler_params=pltpu.CompilerParams(vmem_limit_bytes=24 * 1024 * 1024),
        name="update",
    )(place, high, low, part, other_part, near, far, tiles)
    return result.transpose(0, 2, 1, 3)


def solution(mesh):
    return jax.shard_map(
        shards,
        mesh=mesh,
        in_specs=(P(None, "row", None, "col"),),
        out_specs=P(None, "row", None, "col"),
        check_vma=False,
    )
```

```python
import functools

import jax
import jax.numpy as jnp
from jax import lax
from jax.experimental import pallas as pl
from jax.experimental.pallas import tpu as pltpu
from jax.sharding import PartitionSpec as P

TB = 128
ROWS = 8
SIDE = 4
ROW_TILES = 12
COL_TILES = 3
QUARTER = 3
COLS = 32
HIGHEST = lax.Precision.HIGHEST


def col_of(x, y, core):
    return (x * SIDE + y) * 2 + core


def device_of(z, col):
    return z * SIDE * SIDE * 2 + col


def send(value, pairs):
    return lax.ppermute(value, ("row", "col"), pairs)


def inverse_factor(tile):
    lane = lax.broadcasted_iota(jnp.int32, (8, TB), 1)
    sub = lax.broadcasted_iota(jnp.int32, (8, TB), 0)
    groups = TB // 8
    rows = [tile[8 * g : 8 * g + 8, :] for g in range(groups)]

    def across(value, k):
        return jnp.broadcast_to(value[:, k : k + 1], (8, TB))

    def down(value, k):
        return jnp.broadcast_to(value[k : k + 1, :], (8, TB))

    for p in range(groups):
        first = 8 * p
        wide = {g: [across(rows[g], first + k) for k in range(8)] for g in range(p, groups)}
        inside = (lane >= first) & (lane < first + 8)
        rows[p] = jnp.where(inside, jnp.where(lane - first == sub, 1.0, 0.0), rows[p])
        for g in range(p + 1, groups):
            rows[g] = jnp.where(inside, 0.0, rows[g])
        mine = wide[p]
        coef = {}
        scale = []
        top = []
        for k in range(8):
            r = lax.rsqrt(down(mine[k], k))
            scale.append(r)
            column = jnp.where(sub > k, mine[k] * r, 0.0)
            for m in range(k + 1, 8):
                coef[k, m] = down(mine[m], k) * r
                mine[m] = mine[m] - column * coef[k, m]
            u = down(rows[p], k) * r
            top.append(u)
            rows[p] = jnp.where(sub == k, u, rows[p] - column * u)
        for g in range(p + 1, groups):
            columns = []
            for k in range(8):
                value = wide[g][k]
                for m in range(k):
                    value = value - columns[m] * coef[m, k]
                columns.append(value * scale[k])
            total = rows[g]
            for k in range(8):
                total = total - columns[k] * top[k]
            rows[g] = total
    return jnp.concatenate([jnp.where(lane <= sub + 8 * g, rows[g], 0.0) for g in range(groups)], axis=0)


def halves(value):
    high = value.astype(jnp.bfloat16)
    return high, (value - high.astype(jnp.float32)).astype(jnp.bfloat16)


def product(a, b, transposed):
    dims = (((1,), (1 if transposed else 0,)), ((), ()))
    dot = functools.partial(lax.dot_general, dimension_numbers=dims, preferred_element_type=jnp.float32)
    return dot(a[0], b[0]) + (dot(a[0], b[1]) + dot(a[1], b[0]))


def exact(a, b, transposed=False):
    dims = (((1,), (1 if transposed else 0,)), ((), ()))
    return lax.dot_general(a, b, dims, precision=HIGHEST, preferred_element_type=jnp.float32)


def first_block(place, own, by_row, by_core, inv00, below, schur):
    odd_row = lax.rem(place[0], 2) == 1
    odd_col = lax.rem(place[1], 2) == 1
    left = jnp.where(odd_col, by_core[...], own[...])
    right = jnp.where(odd_col, own[...], by_core[...])
    inv = inverse_factor(jnp.where(odd_row, by_row[...], left))
    l10 = exact(jnp.where(odd_row, left, right.T), inv, transposed=True)
    schur[...] = jnp.where(odd_row, right, by_row[...]) - exact(l10, l10, transposed=True)
    below[...] = l10
    inv00[...] = inv


def second_block(inv00, below, schur, high, low):
    mixed = exact(below[...], inv00[...])
    inv11 = inverse_factor(schur[...])
    inv10 = -exact(inv11, mixed)
    zero = jnp.zeros((TB, TB), jnp.float32)
    for i, line in enumerate(((inv00[...], zero), (inv10, inv11))):
        for j, value in enumerate(line):
            part = slice(i * TB, (i + 1) * TB), slice(j * TB, (j + 1) * TB)
            high[part], low[part] = halves(value)


def update(place, high, low, part, other_part, near, far, kernel, out, block, sem, sems):
    my_row, my_col = place[0], place[1]
    load = pltpu.make_async_copy(kernel, block, sem)
    load.start()
    odd_row = lax.rem(my_row, 2) == 1
    my_x = my_col // (2 * SIDE)
    my_y = lax.rem(my_col // 2, SIDE)
    swapped = lax.rem(my_col, 2) == 1
    inv = high[...], low[...]
    top = jnp.concatenate(
        [
            jnp.concatenate([jnp.where(odd_row, other_part[t], part[t]) for t in range(COL_TILES)], axis=1),
            jnp.concatenate([jnp.where(odd_row, part[t], other_part[t]) for t in range(COL_TILES)], axis=1),
        ],
        axis=0,
    )
    right = halves(product(inv, halves(top), False))
    lane = lax.broadcasted_iota(jnp.int32, (TB, TB), 1)
    sub = lax.broadcasted_iota(jnp.int32, (TB, TB), 0)

    load.wait()
    for quarter in range(SIDE):
        from_x = lax.rem(my_x - quarter + SIDE, SIDE)
        from_y = lax.rem(my_y - quarter + SIDE, SIDE)
        zero = jnp.where(swapped, far[from_x], near[from_x]).reshape(QUARTER * TB, TB)
        one = jnp.where(swapped, near[from_y], far[from_y]).reshape(QUARTER * TB, TB)
        left = product(halves(jnp.concatenate([zero, one], axis=1)), inv, True)
        change = product(halves(left), right, False)
        for i in range(QUARTER):
            s = quarter * QUARTER + i
            rows = slice(i * TB, (i + 1) * TB)
            for t in range(COL_TILES):
                value = block[s, t] - change[rows, t * TB : (t + 1) * TB]
                if t == 0:
                    panel = jnp.where(my_col == 0, left[rows, :TB], left[rows, TB:])
                    value = jnp.where(my_col < 2, panel, value)
                if s == 0:
                    tile_col = t * COLS + my_col
                    value = jnp.where((my_row < 2) & (tile_col > my_row), 0.0, value)
                    value = jnp.where((my_row < 2) & (tile_col == my_row) & (lane > sub), 0.0, value)
                block[s, t] = value
            pltpu.make_async_copy(block.at[s], out.at[s], sems.at[s]).start()
    for s in range(ROW_TILES):
        pltpu.make_async_copy(block.at[s], out.at[s], sems.at[s]).wait()


def after(value, *others):
    return lax.optimization_barrier((value, *others))[0]


def shards(kernel):
    my_row = lax.axis_index("row").astype(jnp.int32)
    my_col = lax.axis_index("col").astype(jnp.int32)
    my_x = my_col // (2 * SIDE)
    my_y = (my_col // 2) % SIDE
    my_core = my_col % 2
    tiles = kernel.transpose(0, 2, 1, 3)
    place = jnp.stack([my_row, my_col])

    zs = range(ROWS)
    sides = range(SIDE)
    cores = range(2)
    cols = range(2 * SIDE * SIDE)

    def at(z, u, v, core):
        return device_of(z, col_of(u, v, core) if core == 0 else col_of(v, u, core))

    def plane_pairs(planes, us, vs, du, dv):
        return [
            (at(z, u, v, c), at(z, (u + du) % SIDE, (v + dv) % SIDE, c)) for z in planes for u in us for v in vs for c in cores
        ]

    def z_pairs(planes, step, columns):
        return [(device_of(z, c), device_of(z + step, c)) for z in planes for c in columns]

    my_u = jnp.where(my_core == 0, my_x, my_y)
    my_v = jnp.where(my_core == 0, my_y, my_x)
    swap_core = [(device_of(z, c), device_of(z, c ^ 1)) for z in zs for c in cols]
    swap_row = [(device_of(z, c), device_of(z ^ 1, c)) for z in zs for c in cols]
    low_planes = (0, 1)

    column = tiles[:, 0].reshape(SIDE, QUARTER, TB, TB)
    head = tiles[0]
    diag = lax.optimization_barrier((head[0], column))[0]
    got = send(diag, plane_pairs(low_planes, (0,), (0,), 2, 0))
    quarter1 = send(column[1], plane_pairs(zs, (0,), (0,), 1, 0))
    quarter3 = send(column[3], plane_pairs(zs, (0,), (0,), 3, 0))
    diag1 = jnp.where(my_u == 2, got, diag)

    got = send(diag1, plane_pairs(low_planes, (0, 2), (0,), 1, 0))
    quarter2 = send(after(column[2], diag1), plane_pairs(zs, (0,), (0,), 2, 0))
    part = after(head, diag1)
    part_got = send(part, z_pairs(low_planes, 4, cols))
    diag2 = jnp.where(my_u % 2 == 1, got, diag1)

    got = send(diag2, plane_pairs(low_planes, sides, (0,), 0, 2))
    diag3 = jnp.where(my_v == 2, got, diag2)

    got = send(diag3, plane_pairs(low_planes, sides, (0, 2), 0, 1))
    quarter1, quarter2, quarter3 = (after(q, diag3) for q in (quarter1, quarter2, quarter3))
    piece = jnp.where(my_u == 0, column[0], jnp.where(my_u == 1, quarter1, jnp.where(my_u == 2, quarter2, quarter3)))
    far_piece = send(piece, plane_pairs(zs, sides, (0,), 0, 2))
    diag4 = jnp.where(my_v % 2 == 1, got, diag3)

    got = send(diag4, z_pairs(low_planes, 4, cols))
    diag5 = jnp.where((my_row == 4) | (my_row == 5), got, diag4)

    got = send(diag5, z_pairs((0, 1, 4, 5), 2, cols))
    part = jnp.where((my_row == 4) | (my_row == 5), after(part_got, diag5), part)
    part_got = send(part, z_pairs((0, 1, 4, 5), 2, cols))
    diag6 = jnp.where(my_row % 4 >= 2, got, diag5)

    by_core = send(diag6, swap_core)
    by_row = send(jnp.where(my_row % 2 == my_core, diag6, by_core), swap_row)
    piece = jnp.where(my_v == 2, after(far_piece, diag5), piece)
    piece1 = send(piece, plane_pairs(zs, sides, (0, 2), 0, 1))
    piece = jnp.where(my_v % 2 == 1, after(piece1, diag6), piece)
    across = send(piece, plane_pairs(zs, sides, sides, 2, 0))
    up = send(piece, plane_pairs(zs, sides, sides, 1, 0))
    down = send(piece, plane_pairs(zs, sides, sides, 3, 0))

    part = jnp.where(my_row % 4 >= 2, part_got, part)
    other_part = send(part, swap_row)
    diag6 = after(diag6, part)

    vmem = pl.BlockSpec(memory_space=pltpu.VMEM)
    smem = pl.BlockSpec(memory_space=pltpu.SMEM)
    anywhere = pl.BlockSpec(memory_space=pl.ANY)
    tile = jax.ShapeDtypeStruct((TB, TB), jnp.float32)
    inverse = jax.ShapeDtypeStruct((2 * TB, 2 * TB), jnp.bfloat16)
    inv00, below, schur = pl.pallas_call(
        first_block,
        out_shape=[tile] * 3,
        in_specs=[smem] + [vmem] * 3,
        out_specs=[vmem] * 3,
        compiler_params=pltpu.CompilerParams(vmem_limit_bytes=8 * 1024 * 1024),
        name="first_block",
    )(place, diag6, by_row, by_core)

    up, down, across = (after(q, schur) for q in (up, down, across))
    near = jnp.stack([piece, up, across, down])
    far = send(near, swap_core)
    high, low = pl.pallas_call(
        second_block,
        out_shape=[inverse] * 2,
        in_specs=[vmem] * 3,
        out_specs=[vmem] * 2,
        compiler_params=pltpu.CompilerParams(vmem_limit_bytes=8 * 1024 * 1024),
        name="second_block",
    )(inv00, below, schur)

    far, other_part = (after(q, high) for q in (far, other_part))
    result = pl.pallas_call(
        update,
        out_shape=jax.ShapeDtypeStruct(tiles.shape, tiles.dtype),
        in_specs=[smem] + [vmem] * 6 + [anywhere],
        out_specs=anywhere,
        scratch_shapes=[
            pltpu.VMEM((ROW_TILES, COL_TILES, TB, TB), jnp.float32),
            pltpu.SemaphoreType.DMA,
            pltpu.SemaphoreType.DMA((ROW_TILES,)),
        ],
        compiler_params=pltpu.CompilerParams(vmem_limit_bytes=24 * 1024 * 1024),
        name="update",
    )(place, high, low, part, other_part, near, far, tiles)
    return result.transpose(0, 2, 1, 3)


def solution(mesh):
    return jax.shard_map(
        shards,
        mesh=mesh,
        in_specs=(P(None, "row", None, "col"),),
        out_specs=P(None, "row", None, "col"),
        check_vma=False,
    )
```

```python
import functools

import jax
import jax.numpy as jnp
from jax import lax
from jax.experimental import pallas as pl
from jax.experimental.pallas import tpu as pltpu
from jax.sharding import PartitionSpec as P

TB = 128
ROWS = 8
SIDE = 4
ROW_TILES = 12
COL_TILES = 3
QUARTER = 3
COLS = 32
HIGHEST = lax.Precision.HIGHEST


def col_of(x, y, core):
    return (x * SIDE + y) * 2 + core


def device_of(z, col):
    return z * SIDE * SIDE * 2 + col


def send(value, pairs):
    return lax.ppermute(value, ("row", "col"), pairs)


def inverse_factor(tile):
    lane = lax.broadcasted_iota(jnp.int32, (8, TB), 1)
    sub = lax.broadcasted_iota(jnp.int32, (8, TB), 0)
    groups = TB // 8
    rows = [tile[8 * g : 8 * g + 8, :] for g in range(groups)]

    def across(value, k):
        return jnp.broadcast_to(value[:, k : k + 1], (8, TB))

    def down(value, k):
        return jnp.broadcast_to(value[k : k + 1, :], (8, TB))

    for p in range(groups):
        first = 8 * p
        wide = {g: [across(rows[g], first + k) for k in range(8)] for g in range(p, groups)}
        inside = (lane >= first) & (lane < first + 8)
        rows[p] = jnp.where(inside, jnp.where(lane - first == sub, 1.0, 0.0), rows[p])
        for g in range(p + 1, groups):
            rows[g] = jnp.where(inside, 0.0, rows[g])
        mine = wide[p]
        coef = {}
        scale = []
        top = []
        for k in range(8):
            r = lax.rsqrt(down(mine[k], k))
            scale.append(r)
            column = jnp.where(sub > k, mine[k] * r, 0.0)
            for m in range(k + 1, 8):
                coef[k, m] = down(mine[m], k) * r
                mine[m] = mine[m] - column * coef[k, m]
            u = down(rows[p], k) * r
            top.append(u)
            rows[p] = jnp.where(sub == k, u, rows[p] - column * u)
        for g in range(p + 1, groups):
            columns = []
            for k in range(8):
                value = wide[g][k]
                for m in range(k):
                    value = value - columns[m] * coef[m, k]
                columns.append(value * scale[k])
            total = rows[g]
            for k in range(8):
                total = total - columns[k] * top[k]
            rows[g] = total
    return jnp.concatenate([jnp.where(lane <= sub + 8 * g, rows[g], 0.0) for g in range(groups)], axis=0)


def halves(value):
    high = value.astype(jnp.bfloat16)
    return high, (value - high.astype(jnp.float32)).astype(jnp.bfloat16)


def product(a, b, transposed):
    dims = (((1,), (1 if transposed else 0,)), ((), ()))
    dot = functools.partial(lax.dot_general, dimension_numbers=dims, preferred_element_type=jnp.float32)
    return dot(a[0], b[0]) + (dot(a[0], b[1]) + dot(a[1], b[0]))


def exact(a, b, transposed=False):
    dims = (((1,), (1 if transposed else 0,)), ((), ()))
    return lax.dot_general(a, b, dims, precision=HIGHEST, preferred_element_type=jnp.float32)


def first_block(place, own, by_row, by_core, inv00, below, schur):
    odd_row = lax.rem(place[0], 2) == 1
    odd_col = lax.rem(place[1], 2) == 1
    left = jnp.where(odd_col, by_core[...], own[...])
    right = jnp.where(odd_col, own[...], by_core[...])
    inv = inverse_factor(jnp.where(odd_row, by_row[...], left))
    l10 = exact(jnp.where(odd_row, left, right.T), inv, transposed=True)
    schur[...] = jnp.where(odd_row, right, by_row[...]) - exact(l10, l10, transposed=True)
    below[...] = l10
    inv00[...] = inv


def second_block(inv00, below, schur, high, low):
    mixed = halves(product(halves(below[...]), halves(inv00[...]), False))
    inv11 = inverse_factor(schur[...])
    inv10 = -product(halves(inv11), mixed, False)
    zero = jnp.zeros((TB, TB), jnp.float32)
    for i, line in enumerate(((inv00[...], zero), (inv10, inv11))):
        for j, value in enumerate(line):
            part = slice(i * TB, (i + 1) * TB), slice(j * TB, (j + 1) * TB)
            high[part], low[part] = halves(value)


def update(place, high, low, part, other_part, near, far, kernel, out, block, sem, sems):
    my_row, my_col = place[0], place[1]
    load = pltpu.make_async_copy(kernel, block, sem)
    load.start()
    odd_row = lax.rem(my_row, 2) == 1
    my_x = my_col // (2 * SIDE)
    my_y = lax.rem(my_col // 2, SIDE)
    swapped = lax.rem(my_col, 2) == 1
    inv = high[...], low[...]
    top = jnp.concatenate(
        [
            jnp.concatenate([jnp.where(odd_row, other_part[t], part[t]) for t in range(COL_TILES)], axis=1),
            jnp.concatenate([jnp.where(odd_row, part[t], other_part[t]) for t in range(COL_TILES)], axis=1),
        ],
        axis=0,
    )
    right = halves(product(inv, halves(top), False))
    lane = lax.broadcasted_iota(jnp.int32, (TB, TB), 1)
    sub = lax.broadcasted_iota(jnp.int32, (TB, TB), 0)

    load.wait()
    for quarter in range(SIDE):
        from_x = lax.rem(my_x - quarter + SIDE, SIDE)
        from_y = lax.rem(my_y - quarter + SIDE, SIDE)
        zero = jnp.where(swapped, far[from_x], near[from_x]).reshape(QUARTER * TB, TB)
        one = jnp.where(swapped, near[from_y], far[from_y]).reshape(QUARTER * TB, TB)
        left = product(halves(jnp.concatenate([zero, one], axis=1)), inv, True)
        change = product(halves(left), right, False)
        for i in range(QUARTER):
            s = quarter * QUARTER + i
            rows = slice(i * TB, (i + 1) * TB)
            for t in range(COL_TILES):
                value = block[s, t] - change[rows, t * TB : (t + 1) * TB]
                if t == 0:
                    panel = jnp.where(my_col == 0, left[rows, :TB], left[rows, TB:])
                    value = jnp.where(my_col < 2, panel, value)
                if s == 0:
                    tile_col = t * COLS + my_col
                    value = jnp.where((my_row < 2) & (tile_col > my_row), 0.0, value)
                    value = jnp.where((my_row < 2) & (tile_col == my_row) & (lane > sub), 0.0, value)
                block[s, t] = value
            pltpu.make_async_copy(block.at[s], out.at[s], sems.at[s]).start()
    for s in range(ROW_TILES):
        pltpu.make_async_copy(block.at[s], out.at[s], sems.at[s]).wait()


def after(value, *others):
    return lax.optimization_barrier((value, *others))[0]


def shards(kernel):
    my_row = lax.axis_index("row").astype(jnp.int32)
    my_col = lax.axis_index("col").astype(jnp.int32)
    my_x = my_col // (2 * SIDE)
    my_y = (my_col // 2) % SIDE
    my_core = my_col % 2
    tiles = kernel.transpose(0, 2, 1, 3)
    place = jnp.stack([my_row, my_col])

    zs = range(ROWS)
    sides = range(SIDE)
    cores = range(2)
    cols = range(2 * SIDE * SIDE)

    def at(z, u, v, core):
        return device_of(z, col_of(u, v, core) if core == 0 else col_of(v, u, core))

    def plane_pairs(planes, us, vs, du, dv):
        return [
            (at(z, u, v, c), at(z, (u + du) % SIDE, (v + dv) % SIDE, c)) for z in planes for u in us for v in vs for c in cores
        ]

    def z_pairs(planes, step, columns):
        return [(device_of(z, c), device_of(z + step, c)) for z in planes for c in columns]

    my_u = jnp.where(my_core == 0, my_x, my_y)
    my_v = jnp.where(my_core == 0, my_y, my_x)
    swap_core = [(device_of(z, c), device_of(z, c ^ 1)) for z in zs for c in cols]
    swap_row = [(device_of(z, c), device_of(z ^ 1, c)) for z in zs for c in cols]
    low_planes = (0, 1)

    column = tiles[:, 0].reshape(SIDE, QUARTER, TB, TB)
    head = tiles[0]
    diag = lax.optimization_barrier((head[0], column))[0]
    got = send(diag, plane_pairs(low_planes, (0,), (0,), 2, 0))
    quarter1 = send(column[1], plane_pairs(zs, (0,), (0,), 1, 0))
    quarter3 = send(column[3], plane_pairs(zs, (0,), (0,), 3, 0))
    diag1 = jnp.where(my_u == 2, got, diag)

    got = send(diag1, plane_pairs(low_planes, (0, 2), (0,), 1, 0))
    quarter2 = send(after(column[2], diag1), plane_pairs(zs, (0,), (0,), 2, 0))
    part = after(head, diag1)
    part_got = send(part, z_pairs(low_planes, 4, cols))
    diag2 = jnp.where(my_u % 2 == 1, got, diag1)

    got = send(diag2, plane_pairs(low_planes, sides, (0,), 0, 2))
    diag3 = jnp.where(my_v == 2, got, diag2)

    got = send(diag3, plane_pairs(low_planes, sides, (0, 2), 0, 1))
    quarter1, quarter2, quarter3 = (after(q, diag3) for q in (quarter1, quarter2, quarter3))
    piece = jnp.where(my_u == 0, column[0], jnp.where(my_u == 1, quarter1, jnp.where(my_u == 2, quarter2, quarter3)))
    far_piece = send(piece, plane_pairs(zs, sides, (0,), 0, 2))
    diag4 = jnp.where(my_v % 2 == 1, got, diag3)

    got = send(diag4, z_pairs(low_planes, 4, cols))
    diag5 = jnp.where((my_row == 4) | (my_row == 5), got, diag4)

    got = send(diag5, z_pairs((0, 1, 4, 5), 2, cols))
    part = jnp.where((my_row == 4) | (my_row == 5), after(part_got, diag5), part)
    part_got = send(part, z_pairs((0, 1, 4, 5), 2, cols))
    diag6 = jnp.where(my_row % 4 >= 2, got, diag5)

    by_core = send(diag6, swap_core)
    by_row = send(jnp.where(my_row % 2 == my_core, diag6, by_core), swap_row)
    piece = jnp.where(my_v == 2, after(far_piece, diag5), piece)
    piece1 = send(piece, plane_pairs(zs, sides, (0, 2), 0, 1))
    piece = jnp.where(my_v % 2 == 1, after(piece1, diag6), piece)
    across = send(piece, plane_pairs(zs, sides, sides, 2, 0))
    up = send(piece, plane_pairs(zs, sides, sides, 1, 0))
    down = send(piece, plane_pairs(zs, sides, sides, 3, 0))

    part = jnp.where(my_row % 4 >= 2, part_got, part)
    other_part = send(part, swap_row)
    diag6 = after(diag6, part)

    vmem = pl.BlockSpec(memory_space=pltpu.VMEM)
    smem = pl.BlockSpec(memory_space=pltpu.SMEM)
    anywhere = pl.BlockSpec(memory_space=pl.ANY)
    tile = jax.ShapeDtypeStruct((TB, TB), jnp.float32)
    inverse = jax.ShapeDtypeStruct((2 * TB, 2 * TB), jnp.bfloat16)
    inv00, below, schur = pl.pallas_call(
        first_block,
        out_shape=[tile] * 3,
        in_specs=[smem] + [vmem] * 3,
        out_specs=[vmem] * 3,
        compiler_params=pltpu.CompilerParams(vmem_limit_bytes=8 * 1024 * 1024),
        name="first_block",
    )(place, diag6, by_row, by_core)

    up, down, across = (after(q, schur) for q in (up, down, across))
    near = jnp.stack([piece, up, across, down])
    far = send(near, swap_core)
    high, low = pl.pallas_call(
        second_block,
        out_shape=[inverse] * 2,
        in_specs=[vmem] * 3,
        out_specs=[vmem] * 2,
        compiler_params=pltpu.CompilerParams(vmem_limit_bytes=8 * 1024 * 1024),
        name="second_block",
    )(inv00, below, schur)

    far, other_part = (after(q, high) for q in (far, other_part))
    result = pl.pallas_call(
        update,
        out_shape=jax.ShapeDtypeStruct(tiles.shape, tiles.dtype),
        in_specs=[smem] + [vmem] * 6 + [anywhere],
        out_specs=anywhere,
        scratch_shapes=[
            pltpu.VMEM((ROW_TILES, COL_TILES, TB, TB), jnp.float32),
            pltpu.SemaphoreType.DMA,
            pltpu.SemaphoreType.DMA((ROW_TILES,)),
        ],
        compiler_params=pltpu.CompilerParams(vmem_limit_bytes=24 * 1024 * 1024),
        name="update",
    )(place, high, low, part, other_part, near, far, tiles)
    return result.transpose(0, 2, 1, 3)


def solution(mesh):
    return jax.shard_map(
        shards,
        mesh=mesh,
        in_specs=(P(None, "row", None, "col"),),
        out_specs=P(None, "row", None, "col"),
        check_vma=False,
    )
```
